32 devices in a mesh: replica: 4 (over y, x), fsdp: 8 (over z, core).
Axes of the slice: x: 2, y: 2, z: 4, core: 2. Of those that a mesh axis runs over, the one named last changes fastest.
Arguments:
- anchor: float32 [3328, 3328], P('fsdp', 'replica'), may hold values from -6 to 6
- prev_delta: bfloat16 [4, 3328, 3328], P('replica', 'fsdp'), may hold values from -4 to 4
- momentum: float32 [3328, 3328], P('fsdp', 'replica'), may hold values from -2 to 2
- pool: bfloat16 [4, 256, 3328], P('replica', 'fsdp'), may hold values from -6 to 6
- ids: int32 [4, 2, 256], P('replica', None, 'fsdp'), may hold values from 0 to 31
- cotangent: bfloat16 [4, 2, 3328, 256], P('replica', None, 'fsdp'), may hold values from -6 to 6
Outputs:
- new_delta: bfloat16 [4, 3328, 3328], P('replica', 'fsdp')
- new_anchor: float32 [3328, 3328], P('fsdp', 'replica')
- new_momentum: float32 [3328, 3328], P('fsdp', 'replica')
The draws below stay inside these ranges and needn't reach their ends.
All inputs are finite; a program needn't handle non-finite values.
Results may differ from the reference program's by a relative error of at most 0.0062.
Values may be sent and summed in bfloat16 or wider, within the bound.
A program may use at most 64 MiB of HBM per device.

```python
import math
import jax
import jax.numpy as jnp
from jax import lax

D = 3328
HW = 3328
STEPS = 2
TOK_DEV = 32
POOL_DEV = 32
ISLANDS = 4
TOK_ISL = 256
ROWS = 256
N_REPLICA = 4
N_FSDP = 8


def level_fields(key, slope_log, row_spread):
    key_rows, key_cols, key_rough_rows, key_rough_cols, key_common = jax.random.split(key, 5)
    row_block = jax.random.uniform(key_rows, (16,), jnp.float32, -1.0, 1.0)
    col_block = jax.random.uniform(key_cols, (16,), jnp.float32, -1.0, 1.0)
    row_index = jnp.arange(HW, dtype=jnp.int32)
    col_index = jnp.arange(D, dtype=jnp.int32)
    row_log = row_spread * row_block[row_index * 16 // HW]
    row_log = row_log + jax.random.uniform(key_rough_rows, (HW,), jnp.float32, -0.35, 0.35)
    col_place = (2.0 * col_index.astype(jnp.float32) + 1.0) / D - 1.0
    col_log = slope_log * col_place + 0.4 * col_block[col_index * 16 // D]
    col_log = col_log + jax.random.uniform(key_rough_cols, (D,), jnp.float32, -0.35, 0.35)
    common = jax.random.normal(key_common, (HW, D), jnp.float32)
    return (jnp.exp(row_log), jnp.exp(col_log), common)


def draw_prev_delta(key, part):
    slope_log, row_spread, common_share, own_share = (0.58, 0.58, 0.25, 0.15)
    row_level, col_level, common = level_fields(key, slope_log, row_spread)
    key = jax.random.fold_in(key, 21)
    key_own, key_pair = jax.random.split(key)
    own_part = jax.random.normal(key_own, (ISLANDS, HW, D), jnp.float32)
    pairing = jax.random.permutation(key_pair, ISLANDS).astype(jnp.int32)
    col_group = jnp.arange(D, dtype=jnp.int32) * ISLANDS // D
    spike_gain = jnp.where(col_group[None, :] == pairing[:, None], 6.0, 1.0).astype(jnp.float32)
    shared_part = row_level[:, None] * col_level[None, :] * common_share * common
    values = shared_part[None] + own_share * row_level[None, :, None] * spike_gain[:, None, :] * own_part
    return jnp.clip(values, -4.0, 4.0).astype(jnp.bfloat16)


def draw_momentum(key, part):
    slope_log, row_spread, common_share = (0.58, 0.58, 0.08)
    row_level, col_level, common = level_fields(key, slope_log, row_spread)
    key = jax.random.fold_in(key, 22)
    own_part = jax.random.normal(key, (HW, D), jnp.float32)
    values = row_level[:, None] * (common_share * col_level[None, :] * common + 0.05 * own_part)
    return jnp.clip(values, -2.0, 2.0)


def with_ends(entries, stream_key, least, largest):
    place = [jax.random.randint(jax.random.fold_in(stream_key, axis), (), 0, length) for axis, length in enumerate(entries.shape)]
    longest = entries.shape.index(max(entries.shape))
    next_to = place[:longest] + [(place[longest] + 1) % entries.shape[longest]] + place[longest + 1:]
    return entries.at[tuple(place)].set(least).at[tuple(next_to)].set(largest)


def shard_levels(key, dims, cuts, low, top_value):
    gain = 1.0
    for dim, shards_of in cuts:
        steps = jax.random.uniform(jax.random.fold_in(jax.random.fold_in(key, 6), dim), (shards_of,), jnp.float32, low / len(cuts), top_value / len(cuts))
        gain = gain * jnp.repeat(jnp.exp(steps), dims[dim] // shards_of).reshape((-1,) + (1,) * (len(dims) - 1 - dim))
    return gain


def bell_draw(stream_key, dims, deviation, reach, cuts=(), held_as=jnp.bfloat16):
    values = jax.random.normal(stream_key, dims, jnp.float32) * deviation
    if len(cuts) > 0:
        values = shard_levels(stream_key, dims, cuts, -0.22, 0.18) * values
    return jnp.clip(values, min=-reach, max=reach).astype(held_as)


def setup_inputs(seed: int = 0) -> dict:
    key_of = jax.random.split(jax.random.key(seed), 7)
    anchor = bell_draw(key_of[0], (HW, D), 1.0, 6.0, ((0, 8), (1, 4)), jnp.float32)
    prev_delta = draw_prev_delta(jax.random.fold_in(key_of[6], 71), 0)
    momentum = draw_momentum(jax.random.fold_in(key_of[6], 71), 0)
    pool = bell_draw(key_of[3], (ISLANDS, ROWS, D), 1.0, 6.0, ((0, 4), (1, 8)))
    ids = with_ends(jax.random.randint(key_of[4], (ISLANDS, STEPS, TOK_ISL), 0, POOL_DEV), jax.random.fold_in(key_of[4], 1), 0, POOL_DEV - 1).astype(jnp.int32)
    cotangent = bell_draw(key_of[5], (ISLANDS, STEPS, HW, TOK_ISL), 1.0, 6.0, ((0, 4), (2, 8)))
    return {"anchor": anchor, "prev_delta": prev_delta, "momentum": momentum, "pool": pool, "ids": ids, "cotangent": cotangent}


INNER_RATE = 2.0
INNER_DECAY = 0.1
PENALTY = 0.5
MOMENT_DECAY = 0.9
OUTER_RATE = 0.7
CLIP_SHARE = 0.05

def silu_slope(preact):
    sigmoid_val = jax.nn.sigmoid(preact)
    return sigmoid_val * (1.0 + preact * (1.0 - sigmoid_val))

def reference(anchor, prev_delta, momentum, pool, ids, cotangent):
    root_width = math.sqrt(D)
    base_rows = jnp.arange(TOK_DEV * N_FSDP, dtype=jnp.int32) // TOK_DEV * POOL_DEV
    deltas = []
    for island in range(N_REPLICA):
        weights = anchor
        for inner_step in range(STEPS):
            batch = pool[island][base_rows + ids[island, inner_step]]
            rounded = weights.astype(jnp.bfloat16)
            preact = jnp.dot(rounded, batch.T, preferred_element_type=jnp.float32) / root_width
            scaled = (cotangent[island, inner_step].astype(jnp.float32) * silu_slope(preact)).astype(jnp.bfloat16)
            gradient = jnp.dot(scaled, batch, preferred_element_type=jnp.float32) / root_width
            weights = weights - INNER_RATE * gradient - INNER_DECAY * weights
        deltas.append((anchor - weights).astype(jnp.bfloat16))
    new_delta = jnp.stack(deltas)
    averaged = lax.optimization_barrier(jnp.sum(prev_delta.astype(jnp.float32), axis=0)) / N_REPLICA
    corrected = averaged + PENALTY * (averaged - momentum)
    squares = jnp.sum(corrected * corrected)
    max_norm = CLIP_SHARE * math.sqrt(D * HW)
    factor = jnp.minimum(1.0, max_norm / jnp.sqrt(squares + 1e-06))
    clipped = factor * corrected
    new_momentum = MOMENT_DECAY * momentum + clipped
    new_anchor = anchor - OUTER_RATE * (MOMENT_DECAY * new_momentum + clipped)
    return (new_delta, new_anchor, new_momentum)
```

```python
import functools
import math

import jax
import jax.numpy as jnp
from jax import lax
from jax.experimental import pallas as pl
from jax.experimental.pallas import tpu as pltpu
from jax.sharding import PartitionSpec as P

D = 3328
HW = 3328


INNER_RATE = 2.0
INNER_DECAY = 0.1
PENALTY = 0.5
MOMENT_DECAY = 0.9
OUTER_RATE = 0.7
CLIP_SHARE = 0.05


def silu_slope(preact):
    sigmoid_val = jax.nn.sigmoid(preact)
    return sigmoid_val * (1.0 + preact * (1.0 - sigmoid_val))


def row_gradient(portion, rounded, cot_step, root_width):
    preact = (
        lax.dot_general(
            rounded, portion, (((1,), (1,)), ((), ())), preferred_element_type=jnp.float32
        )
        / root_width
    )
    scaled = (cot_step.astype(jnp.float32) * silu_slope(preact)).astype(jnp.bfloat16)
    return jnp.dot(scaled, portion, preferred_element_type=jnp.float32)


def island_mean(prev_delta):
    summed = lax.psum_scatter(
        prev_delta[0].astype(jnp.float32).astype(jnp.bfloat16),
        "replica",
        scatter_dimension=1,
        tiled=True,
    ).astype(jnp.float32)
    return summed / lax.axis_size("replica")


def plain_body(anchor, prev_delta, momentum, pool, ids, cotangent):
    root_width = math.sqrt(D)
    anchor_island = lax.all_gather(anchor, "replica", axis=1, tiled=True)
    own_rows = jnp.take(pool[0], ids[0], axis=0)
    weights = anchor_island
    zero_grad = jnp.zeros(anchor_island.shape, jnp.float32)
    for inner_step in range(ids.shape[1]):
        rounded = weights.astype(jnp.bfloat16)
        cot_step = cotangent[0, inner_step]

        def accumulate(running, portion, first, rounded=rounded, cot_step=cot_step):
            return row_gradient(portion, rounded, cot_step, root_width)

        gradient = accumulate(
            zero_grad,
            lax.all_gather(own_rows[inner_step], "fsdp", axis=0, tiled=True),
            jnp.int32(0),
        )
        weights = weights - INNER_RATE * (gradient / root_width) - INNER_DECAY * weights
    new_delta = (anchor_island - weights).astype(jnp.bfloat16)[None]
    averaged = island_mean(prev_delta)
    corrected = averaged + PENALTY * (averaged - momentum)
    squares = lax.psum(jnp.sum(corrected * corrected), ("replica", "fsdp"))
    max_norm = CLIP_SHARE * math.sqrt(D * HW)
    factor = jnp.minimum(1.0, max_norm / jnp.sqrt(squares + 1e-06))
    clipped = factor * corrected
    new_momentum = MOMENT_DECAY * momentum + clipped
    new_anchor = anchor - OUTER_RATE * (MOMENT_DECAY * new_momentum + clipped)
    return (new_delta, new_anchor, new_momentum)


def contract_last(left, right):
    return lax.dot_general(
        left, right, (((1,), (1,)), ((), ())), preferred_element_type=jnp.float32
    )


def exchange_kernel(
    n_fsdp,
    ids_ref, prev_ref, anchor_ref, mom_ref, pool_ref, cot_ref,
    ag_out, bb_out, corr_out, scaled_out, sq_out,
    pv, blk, av, mv, plv, cv, ag, poolb, selb, bb, xr, yr, qs, s2, corr, preact, gram, sqv,
    local_sem, out_sem, send_sem, recv_sem, pool_send, pool_recv, sel_send, sel_recv,
):
    r = lax.axis_index("replica")
    f = lax.axis_index("fsdp")
    rx = r + 1 - 2 * (r % 2)
    ry = r + 2 - 4 * (r // 2)
    rd = 3 - r
    fs = f + 1 - 2 * (f % 2)
    hops = list(range(1, n_fsdp // 2))
    x_dev, y_dev, sib_dev = (rx, f), (ry, f), (r, fs)
    z_to = {k: (r, (f + 2 * k) % n_fsdp) for k in hops}
    rows, width = anchor_ref.shape
    half = rows // 2
    tok = poolb.shape[2]
    n_tok = n_fsdp * tok
    root_width = math.sqrt(pv.shape[1])
    lower, upper = pl.ds(0, half), pl.ds(half, half)

    def local(src, dst, index):
        copy = pltpu.make_async_copy(src, dst, local_sem.at[index])
        copy.start()
        return copy

    def remote(src, dst, index, dev, sends=send_sem, recvs=recv_sem):
        return pltpu.make_async_remote_copy(
            src_ref=src,
            dst_ref=dst,
            send_sem=sends.at[index],
            recv_sem=recvs.at[index],
            device_id=dev,
            device_id_type=pl.DeviceIdType.MESH,
        )

    in_pool = local(pool_ref.at[0], plv, 0)
    in_low = local(prev_ref.at[0, lower], pv.at[lower], 1)
    in_up = local(prev_ref.at[0, upper], pv.at[upper], 2)
    in_anchor = local(anchor_ref, av, 3)
    in_mom = local(mom_ref, mv, 4)
    in_cot = local(cot_ref.at[0], cv, 5)

    barrier = pltpu.get_barrier_semaphore()
    partners = [x_dev, y_dev, sib_dev] + [z_to[k] for k in hops]
    for dev in partners:
        pl.semaphore_signal(barrier, inc=1, device_id=dev, device_id_type=pl.DeviceIdType.MESH)

    in_low.wait()
    for j in range(4):
        blk[j, lower, :] = pv[lower, width * j : width * (j + 1)]
    pl.semaphore_wait(barrier, len(partners))
    started = []

    def send(src, dst, index, dev):
        copy = remote(src, dst, index, dev)
        copy.start()
        started.append(copy)
        return copy

    rs_xd = send(blk.at[rd, lower], xr.at[0], 0, x_dev)
    rs_xo = send(blk.at[rx, lower], xr.at[1], 1, x_dev)
    in_up.wait()
    for j in range(4):
        blk[j, upper, :] = pv[upper, width * j : width * (j + 1)]
    rs_yd = send(blk.at[rd, upper], yr.at[0], 2, y_dev)
    rs_yo = send(blk.at[ry, upper], yr.at[1], 3, y_dev)

    in_pool.wait()
    for j in range(4):
        poolb[f, j] = plv[:, width * j : width * (j + 1)]
    square = (tok, tok)
    eye = lax.broadcasted_iota(jnp.int32, square, 0) == lax.broadcasted_iota(jnp.int32, square, 1)
    lane = lax.broadcasted_iota(jnp.int32, (tok, n_tok), 1).astype(jnp.float32)
    base = (f * tok).astype(jnp.float32)
    for k in range(2):
        chosen = jnp.broadcast_to(ids_ref[0, k : k + 1, :].astype(jnp.float32), square)
        column = jnp.sum(jnp.where(eye, chosen, 0.0), axis=1, keepdims=True)
        selb[f, k] = jnp.where(lane == column + base, 1.0, 0.0).astype(jnp.bfloat16)

    pool_moves = []

    def pool_move(slot, index, dev):
        for buf, sends, recvs in ((poolb, pool_send, pool_recv), (selb, sel_send, sel_recv)):
            copy = remote(buf.at[slot], buf.at[slot], index, dev, sends, recvs)
            copy.start()
            pool_moves.append(copy)

    def pool_arrival(slot, index, dev):
        for buf, sends, recvs in ((poolb, pool_send, pool_recv), (selb, sel_send, sel_recv)):
            remote(buf.at[slot], buf.at[slot], index, dev, sends, recvs).wait_recv()

    for k in hops:
        pool_move(f, k, z_to[k])
    n_line = n_fsdp // 2
    pool_move(f, n_line, sib_dev)

    in_anchor.wait()
    ag[r] = av[...].astype(jnp.bfloat16)
    send(ag.at[r, lower], ag.at[r, lower], 6, x_dev)
    send(ag.at[r, upper], ag.at[r, upper], 7, y_dev)

    rs_xd.wait_recv()
    qs[0] = (blk[ry, lower, :].astype(jnp.float32) + xr[0].astype(jnp.float32)).astype(jnp.bfloat16)
    s2_y = send(qs.at[0], s2.at[0], 4, y_dev)
    rs_yd.wait_recv()
    qs[1] = (blk[rx, upper, :].astype(jnp.float32) + yr[0].astype(jnp.float32)).astype(jnp.bfloat16)
    s2_x = send(qs.at[1], s2.at[1], 5, x_dev)
    send(ag.at[r, upper], ag.at[r, upper], 8, x_dev)
    send(ag.at[r, lower], ag.at[r, lower], 9, y_dev)

    remote(ag.at[rx, lower], ag.at[rx, lower], 6, x_dev).wait_recv()
    send(ag.at[rx, lower], ag.at[rx, lower], 10, y_dev)
    remote(ag.at[ry, upper], ag.at[ry, upper], 7, y_dev).wait_recv()
    send(ag.at[ry, upper], ag.at[ry, upper], 11, x_dev)

    for k in hops:
        slot = (f + n_fsdp - 2 * k) % n_fsdp
        pool_arrival(slot, k, z_to[k])
        pool_move(slot, n_line + k, sib_dev)

    rs_xo.wait_recv()
    rs_yo.wait_recv()
    in_mom.wait()
    squares = jnp.zeros((), jnp.float32)
    for part, first, second, final in ((lower, xr, 0, s2_y), (upper, yr, 1, s2_x)):
        final.wait_recv()
        total = blk[r, part, :].astype(jnp.float32) + first[1].astype(jnp.float32)
        averaged = (total + s2[second].astype(jnp.float32)) / 4.0
        value = averaged + PENALTY * (averaged - mv[part, :])
        corr[part, :] = value
        squares = squares + jnp.sum(value * value)
    sqv[0] = jnp.full(sqv.shape[1:], squares, jnp.float32)
    outs = []

    def put(src, dst, index):
        copy = pltpu.make_async_copy(src, dst, out_sem.at[index])
        copy.start()
        outs.append(copy)

    put(corr, corr_out, 0)
    put(ag.at[r], ag_out.at[r], 1)

    sq_x = send(sqv.at[0], sqv.at[4], 12, x_dev)

    pool_arrival(fs, n_line, sib_dev)
    for k in hops:
        pool_arrival((fs + n_fsdp - 2 * k) % n_fsdp, n_line + k, sib_dev)

    @pl.loop(0, 4)
    def _(j):
        block = poolb[:, j, :, :].reshape(n_tok, width)
        for k in range(2):
            choice = selb[:, k, :, :].reshape(n_tok, n_tok)
            bb[j, pl.ds(k * n_tok, n_tok), :] = jnp.dot(
                choice, block, preferred_element_type=jnp.float32
            ).astype(jnp.bfloat16)

    put(bb, bb_out, 2)

    sq_x.wait_recv()
    sqv[1] = sqv[0] + sqv[4]
    sq_y = send(sqv.at[1], sqv.at[5], 13, y_dev)

    gram[...] = jnp.zeros_like(gram)

    @pl.loop(0, 4)
    def _(j):
        gram[...] += contract_last(bb[j, pl.ds(0, n_tok), :], bb[j, pl.ds(n_tok, n_tok), :])

    sq_y.wait_recv()
    sqv[2] = sqv[1] + sqv[5]
    sq_s = send(sqv.at[2], sqv.at[6], 14, sib_dev)

    def add_preact(j, fresh):
        @pl.loop(0, 2)
        def _(h):
            part = pl.ds(pl.multiple_of(h * half, half), half)
            value = contract_last(ag[j, part, :], bb[j])
            preact[part, :] = value if fresh else preact[part, :] + value

    add_preact(r, True)

    sq_s.wait_recv()
    sqv[3] = sqv[2] + sqv[6]
    sq_z = [send(sqv.at[3], sqv.at[6 + k], 14 + k, z_to[k]) for k in hops]

    remote(ag.at[rx, upper], ag.at[rx, upper], 8, x_dev).wait_recv()
    put(ag.at[rx], ag_out.at[rx], 3)
    add_preact(rx, False)
    remote(ag.at[ry, lower], ag.at[ry, lower], 9, y_dev).wait_recv()
    put(ag.at[ry], ag_out.at[ry], 4)
    add_preact(ry, False)

    whole = sqv[3]
    for k, copy in zip(hops, sq_z):
        copy.wait_recv()
        whole = whole + sqv[6 + k]
    sq_out[...] = whole

    in_cot.wait()
    gram_high = gram[...].astype(jnp.bfloat16)
    gram_low = (gram[...] - gram_high.astype(jnp.float32)).astype(jnp.bfloat16)

    remote(ag.at[rd, lower], ag.at[rd, lower], 10, y_dev).wait_recv()
    remote(ag.at[rd, upper], ag.at[rd, upper], 11, x_dev).wait_recv()
    put(ag.at[rd], ag_out.at[rd], 5)
    add_preact(rd, False)

    @pl.loop(0, 2)
    def _(h):
        part = pl.ds(pl.multiple_of(h * half, half), half)
        first = preact[part, pl.ds(0, n_tok)] / root_width
        scaled = (cv[0, part, :].astype(jnp.float32) * silu_slope(first)).astype(jnp.bfloat16)
        scaled_out[part, pl.ds(0, n_tok)] = scaled
        moved = jnp.dot(scaled, gram_high, preferred_element_type=jnp.float32)
        moved = moved + jnp.dot(scaled, gram_low, preferred_element_type=jnp.float32)
        second = (1.0 - INNER_DECAY) * preact[part, pl.ds(n_tok, n_tok)]
        second = (second - INNER_RATE * (moved / root_width)) / root_width
        scaled_out[part, pl.ds(n_tok, n_tok)] = (
            cv[1, part, :].astype(jnp.float32) * silu_slope(second)
        ).astype(jnp.bfloat16)

    for copy in started:
        copy.wait_send()
    for copy in pool_moves:
        copy.wait_send()
    for copy in outs:
        copy.wait()


def update_kernel(
    max_norm, root_width,
    ag_ref, bb_ref, scaled_ref, sq_ref, corr_ref, mom_ref, anchor_ref,
    delta_ref, new_anchor_ref, new_mom_ref,
):
    width = ag_ref.shape[2]
    n_tok = bb_ref.shape[1] // 2
    keep = 1.0 - INNER_DECAY
    for b in range(2):
        first = jnp.dot(
            scaled_ref[:, :n_tok], bb_ref[b, :n_tok, :], preferred_element_type=jnp.float32
        )
        second = jnp.dot(
            scaled_ref[:, n_tok:], bb_ref[b, n_tok:, :], preferred_element_type=jnp.float32
        )
        moved = (INNER_RATE * keep / root_width) * first + (INNER_RATE / root_width) * second
        value = (1.0 - keep * keep) * ag_ref[b].astype(jnp.float32) + moved
        delta_ref[0, :, width * b : width * (b + 1)] = value.astype(jnp.bfloat16)
    factor = jnp.minimum(1.0, max_norm / jnp.sqrt(sq_ref[0:1, 0:1] + 1e-06))
    clipped = factor * corr_ref[...]
    new_mom = MOMENT_DECAY * mom_ref[...] + clipped
    new_mom_ref[...] = new_mom
    new_anchor_ref[...] = anchor_ref[...] - OUTER_RATE * (MOMENT_DECAY * new_mom + clipped)


def fast_body(anchor, prev_delta, momentum, pool, ids, cotangent):
    n_fsdp = lax.axis_size("fsdp")
    rows, width = anchor.shape
    full = prev_delta.shape[2]
    tok = pool.shape[1]
    n_tok = tok * n_fsdp
    half = rows // 2
    n_line = n_fsdp // 2
    bf16, f32 = jnp.bfloat16, jnp.float32
    any_spec = pl.BlockSpec(memory_space=pl.ANY)
    vmem_spec = pl.BlockSpec(memory_space=pltpu.VMEM)
    dma = pltpu.SemaphoreType.DMA
    ag, bb, corr, scaled, sq = pl.pallas_call(
        functools.partial(exchange_kernel, n_fsdp),
        out_shape=(
            jax.ShapeDtypeStruct((4, rows, width), bf16),
            jax.ShapeDtypeStruct((4, 2 * n_tok, width), bf16),
            jax.ShapeDtypeStruct((rows, width), f32),
            jax.ShapeDtypeStruct((rows, 2 * n_tok), bf16),
            jax.ShapeDtypeStruct((8, 128), f32),
        ),
        in_specs=[vmem_spec] + [any_spec] * 5,
        out_specs=(any_spec, any_spec, any_spec, vmem_spec, vmem_spec),
        scratch_shapes=[
            pltpu.VMEM((rows, full), bf16),
            pltpu.VMEM((4, rows, width), bf16),
            pltpu.VMEM((rows, width), f32),
            pltpu.VMEM((rows, width), f32),
            pltpu.VMEM((tok, full), bf16),
            pltpu.VMEM((2, rows, n_tok), bf16),
            pltpu.VMEM((4, rows, width), bf16),
            pltpu.VMEM((n_fsdp, 4, tok, width), bf16),
            pltpu.VMEM((n_fsdp, 2, tok, n_tok), bf16),
            pltpu.VMEM((4, 2 * n_tok, width), bf16),
            pltpu.VMEM((2, half, width), bf16),
            pltpu.VMEM((2, half, width), bf16),
            pltpu.VMEM((2, half, width), bf16),
            pltpu.VMEM((2, half, width), bf16),
            pltpu.VMEM((rows, width), f32),
            pltpu.VMEM((rows, 2 * n_tok), f32),
            pltpu.VMEM((n_tok, n_tok), f32),
            pltpu.VMEM((6 + n_line, 8, 128), f32),
            dma((6,)),
            dma((6,)),
            dma((14 + n_line,)),
            dma((14 + n_line,)),
            dma((2 * n_line,)),
            dma((2 * n_line,)),
            dma((2 * n_line,)),
            dma((2 * n_line,)),
        ],
        compiler_params=pltpu.CompilerParams(
            collective_id=0, has_side_effects=True, vmem_limit_bytes=48 * 1024 * 1024
        ),
        name="exchange",
    )(ids, prev_delta, anchor, momentum, pool, cotangent)
    quarter = rows // 4
    by_rows = pl.BlockSpec((quarter, width), lambda c, i: (2 * c + i, 0))
    delta, new_anchor, new_momentum = pl.pallas_call(
        functools.partial(update_kernel, CLIP_SHARE * math.sqrt(D * HW), math.sqrt(D)),
        grid=(2, 2),
        out_shape=(
            jax.ShapeDtypeStruct(prev_delta.shape, bf16),
            jax.ShapeDtypeStruct(anchor.shape, f32),
            jax.ShapeDtypeStruct(anchor.shape, f32),
        ),
        in_specs=[
            pl.BlockSpec((2, half, width), lambda c, i: (c, i, 0)),
            pl.BlockSpec((2, 2 * n_tok, width), lambda c, i: (c, 0, 0)),
            pl.BlockSpec((half, 2 * n_tok), lambda c, i: (i, 0)),
            pl.BlockSpec((8, 128), lambda c, i: (0, 0)),
            by_rows,
            by_rows,
            by_rows,
        ],
        out_specs=(
            pl.BlockSpec((1, half, 2 * width), lambda c, i: (0, i, c)),
            by_rows,
            by_rows,
        ),
        compiler_params=pltpu.CompilerParams(vmem_limit_bytes=48 * 1024 * 1024),
        name="update",
    )(ag, bb, scaled, sq, corr, momentum, anchor)
    return (delta, new_anchor, new_momentum)


def body(anchor, prev_delta, momentum, pool, ids, cotangent):
    rows, width = anchor.shape
    fits = (
        lax.axis_size("replica") == 4
        and lax.axis_size("fsdp") % 2 == 0
        and rows % 32 == 0
        and width % 64 == 0
        and pool.shape[1] % 16 == 0
        and ids.shape[1] == 2
        and ids.shape[2] == pool.shape[1]
        and (ids.shape[2] * lax.axis_size("fsdp")) % 128 == 0
    )
    chosen = fast_body if fits else plain_body
    return chosen(anchor, prev_delta, momentum, pool, ids, cotangent)


def solution(mesh):
    return jax.shard_map(
        body,
        mesh=mesh,
        in_specs=(
            P("fsdp", "replica"),
            P("replica", "fsdp", None),
            P("fsdp", "replica"),
            P("replica", "fsdp", None),
            P("replica", None, "fsdp"),
            P("replica", None, "fsdp", None),
        ),
        out_specs=(P("replica", "fsdp", None), P("fsdp", "replica"), P("fsdp", "replica")),
        check_vma=False,
    )
```

```python
import functools
import math

import jax
import jax.numpy as jnp
from jax import lax
from jax.experimental import pallas as pl
from jax.experimental.pallas import tpu as pltpu
from jax.sharding import PartitionSpec as P

D = 3328
HW = 3328


INNER_RATE = 2.0
INNER_DECAY = 0.1
PENALTY = 0.5
MOMENT_DECAY = 0.9
OUTER_RATE = 0.7
CLIP_SHARE = 0.05


def silu_slope(preact):
    sigmoid_val = jax.nn.sigmoid(preact)
    return sigmoid_val * (1.0 + preact * (1.0 - sigmoid_val))


def row_gradient(portion, rounded, cot_step, root_width):
    preact = (
        lax.dot_general(
            rounded, portion, (((1,), (1,)), ((), ())), preferred_element_type=jnp.float32
        )
        / root_width
    )
    scaled = (cot_step.astype(jnp.float32) * silu_slope(preact)).astype(jnp.bfloat16)
    return jnp.dot(scaled, portion, preferred_element_type=jnp.float32)


def island_mean(prev_delta):
    summed = lax.psum_scatter(
        prev_delta[0].astype(jnp.float32).astype(jnp.bfloat16),
        "replica",
        scatter_dimension=1,
        tiled=True,
    ).astype(jnp.float32)
    return summed / lax.axis_size("replica")


def plain_body(anchor, prev_delta, momentum, pool, ids, cotangent):
    root_width = math.sqrt(D)
    anchor_island = lax.all_gather(anchor, "replica", axis=1, tiled=True)
    own_rows = jnp.take(pool[0], ids[0], axis=0)
    weights = anchor_island
    zero_grad = jnp.zeros(anchor_island.shape, jnp.float32)
    for inner_step in range(ids.shape[1]):
        rounded = weights.astype(jnp.bfloat16)
        cot_step = cotangent[0, inner_step]

        def accumulate(running, portion, first, rounded=rounded, cot_step=cot_step):
            return row_gradient(portion, rounded, cot_step, root_width)

        gradient = accumulate(
            zero_grad,
            lax.all_gather(own_rows[inner_step], "fsdp", axis=0, tiled=True),
            jnp.int32(0),
        )
        weights = weights - INNER_RATE * (gradient / root_width) - INNER_DECAY * weights
    new_delta = (anchor_island - weights).astype(jnp.bfloat16)[None]
    averaged = island_mean(prev_delta)
    corrected = averaged + PENALTY * (averaged - momentum)
    squares = lax.psum(jnp.sum(corrected * corrected), ("replica", "fsdp"))
    max_norm = CLIP_SHARE * math.sqrt(D * HW)
    factor = jnp.minimum(1.0, max_norm / jnp.sqrt(squares + 1e-06))
    clipped = factor * corrected
    new_momentum = MOMENT_DECAY * momentum + clipped
    new_anchor = anchor - OUTER_RATE * (MOMENT_DECAY * new_momentum + clipped)
    return (new_delta, new_anchor, new_momentum)


def contract_last(left, right):
    return lax.dot_general(
        left, right, (((1,), (1,)), ((), ())), preferred_element_type=jnp.float32
    )


def exchange_kernel(
    n_fsdp, max_norm,
    ids_ref, prev_ref, anchor_ref, mom_ref, pool_ref, cot_ref,
    ag_out, pool_out, new_mom_out, new_anchor_out, coef_out,
    pv, blk, av, mv, plv, cv, ag, poolb, selb, bb, xr, yr, qs, s2, corr, preact, gram, sqv,
    local_sem, out_sem, send_sem, recv_sem, pool_send, pool_recv, sel_send, sel_recv,
):
    r = lax.axis_index("replica")
    f = lax.axis_index("fsdp")
    rx = r + 1 - 2 * (r % 2)
    ry = r + 2 - 4 * (r // 2)
    rd = 3 - r
    fs = f + 1 - 2 * (f % 2)
    hops = list(range(1, n_fsdp // 2))
    x_dev, y_dev, sib_dev = (rx, f), (ry, f), (r, fs)
    z_to = {k: (r, (f + 2 * k) % n_fsdp) for k in hops}
    rows, width = anchor_ref.shape
    half = rows // 2
    tok = poolb.shape[2]
    n_tok = n_fsdp * tok
    root_width = math.sqrt(pv.shape[1])
    lower, upper = pl.ds(0, half), pl.ds(half, half)

    def local(src, dst, index):
        copy = pltpu.make_async_copy(src, dst, local_sem.at[index])
        copy.start()
        return copy

    def remote(src, dst, index, dev, sends=send_sem, recvs=recv_sem):
        return pltpu.make_async_remote_copy(
            src_ref=src,
            dst_ref=dst,
            send_sem=sends.at[index],
            recv_sem=recvs.at[index],
            device_id=dev,
            device_id_type=pl.DeviceIdType.MESH,
        )

    in_pool = local(pool_ref.at[0], plv, 0)
    in_low = local(prev_ref.at[0, lower], pv.at[lower], 1)
    in_up = local(prev_ref.at[0, upper], pv.at[upper], 2)
    in_anchor = local(anchor_ref, av, 3)
    in_mom = local(mom_ref, mv, 4)
    in_cot = local(cot_ref.at[0], cv, 5)

    barrier = pltpu.get_barrier_semaphore()
    partners = [x_dev, y_dev, sib_dev] + [z_to[k] for k in hops]
    for dev in partners:
        pl.semaphore_signal(barrier, inc=1, device_id=dev, device_id_type=pl.DeviceIdType.MESH)

    in_low.wait()
    for j in range(4):
        blk[j, lower, :] = pv[lower, width * j : width * (j + 1)]
    pl.semaphore_wait(barrier, len(partners))
    started = []

    def send(src, dst, index, dev):
        copy = remote(src, dst, index, dev)
        copy.start()
        started.append(copy)
        return copy

    rs_xd = send(blk.at[rd, lower], xr.at[0], 0, x_dev)
    rs_xo = send(blk.at[rx, lower], xr.at[1], 1, x_dev)
    in_up.wait()
    for j in range(4):
        blk[j, upper, :] = pv[upper, width * j : width * (j + 1)]
    rs_yd = send(blk.at[rd, upper], yr.at[0], 2, y_dev)
    rs_yo = send(blk.at[ry, upper], yr.at[1], 3, y_dev)

    in_pool.wait()
    for j in range(4):
        poolb[f, j] = plv[:, width * j : width * (j + 1)]
    square = (tok, tok)
    eye = lax.broadcasted_iota(jnp.int32, square, 0) == lax.broadcasted_iota(jnp.int32, square, 1)
    lane = lax.broadcasted_iota(jnp.int32, (tok, n_tok), 1).astype(jnp.float32)
    base = (f * tok).astype(jnp.float32)
    for k in range(2):
        chosen = jnp.broadcast_to(ids_ref[0, k : k + 1, :].astype(jnp.float32), square)
        column = jnp.sum(jnp.where(eye, chosen, 0.0), axis=1, keepdims=True)
        selb[f, k] = jnp.where(lane == column + base, 1.0, 0.0).astype(jnp.bfloat16)

    pool_moves = []

    def pool_move(slot, index, dev):
        for buf, sends, recvs in ((poolb, pool_send, pool_recv), (selb, sel_send, sel_recv)):
            copy = remote(buf.at[slot], buf.at[slot], index, dev, sends, recvs)
            copy.start()
            pool_moves.append(copy)

    def pool_arrival(slot, index, dev):
        for buf, sends, recvs in ((poolb, pool_send, pool_recv), (selb, sel_send, sel_recv)):
            remote(buf.at[slot], buf.at[slot], index, dev, sends, recvs).wait_recv()

    for k in hops:
        pool_move(f, k, z_to[k])
    n_line = n_fsdp // 2
    pool_move(f, n_line, sib_dev)

    in_anchor.wait()
    ag[r] = av[...].astype(jnp.bfloat16)
    send(ag.at[r, lower], ag.at[r, lower], 6, x_dev)
    send(ag.at[r, upper], ag.at[r, upper], 7, y_dev)

    rs_xd.wait_recv()
    qs[0] = (blk[ry, lower, :].astype(jnp.float32) + xr[0].astype(jnp.float32)).astype(jnp.bfloat16)
    s2_y = send(qs.at[0], s2.at[0], 4, y_dev)
    rs_yd.wait_recv()
    qs[1] = (blk[rx, upper, :].astype(jnp.float32) + yr[0].astype(jnp.float32)).astype(jnp.bfloat16)
    s2_x = send(qs.at[1], s2.at[1], 5, x_dev)
    send(ag.at[r, upper], ag.at[r, upper], 8, x_dev)
    send(ag.at[r, lower], ag.at[r, lower], 9, y_dev)

    remote(ag.at[rx, lower], ag.at[rx, lower], 6, x_dev).wait_recv()
    send(ag.at[rx, lower], ag.at[rx, lower], 10, y_dev)
    remote(ag.at[ry, upper], ag.at[ry, upper], 7, y_dev).wait_recv()
    send(ag.at[ry, upper], ag.at[ry, upper], 11, x_dev)

    for k in hops:
        slot = (f + n_fsdp - 2 * k) % n_fsdp
        pool_arrival(slot, k, z_to[k])
        pool_move(slot, n_line + k, sib_dev)

    rs_xo.wait_recv()
    rs_yo.wait_recv()
    in_mom.wait()
    squares = jnp.zeros((), jnp.float32)
    for part, first, second, final in ((lower, xr, 0, s2_y), (upper, yr, 1, s2_x)):
        final.wait_recv()
        total = blk[r, part, :].astype(jnp.float32) + first[1].astype(jnp.float32)
        averaged = (total + s2[second].astype(jnp.float32)) / 4.0
        value = averaged + PENALTY * (averaged - mv[part, :])
        corr[part, :] = value
        squares = squares + jnp.sum(value * value)
    sqv[0] = jnp.full(sqv.shape[1:], squares, jnp.float32)
    outs = []

    def put(src, dst, index):
        copy = pltpu.make_async_copy(src, dst, out_sem.at[index])
        copy.start()
        outs.append(copy)

    put(ag.at[r], ag_out.at[r], 1)

    sq_x = send(sqv.at[0], sqv.at[4], 12, x_dev)

    pool_arrival(fs, n_line, sib_dev)
    for k in hops:
        pool_arrival((fs + n_fsdp - 2 * k) % n_fsdp, n_line + k, sib_dev)

    @pl.loop(0, 4)
    def _(j):
        block = poolb[:, j, :, :].reshape(n_tok, width)
        for k in range(2):
            choice = selb[:, k, :, :].reshape(n_tok, n_tok)
            bb[j, pl.ds(k * n_tok, n_tok), :] = jnp.dot(
                choice, block, preferred_element_type=jnp.float32
            ).astype(jnp.bfloat16)

    put(poolb, pool_out, 2)

    sq_x.wait_recv()
    sqv[1] = sqv[0] + sqv[4]
    sq_y = send(sqv.at[1], sqv.at[5], 13, y_dev)

    gram[...] = jnp.zeros_like(gram)

    @pl.loop(0, 4)
    def _(j):
        gram[...] += contract_last(bb[j, pl.ds(0, n_tok), :], bb[j, pl.ds(n_tok, n_tok), :])

    sq_y.wait_recv()
    sqv[2] = sqv[1] + sqv[5]
    sq_s = send(sqv.at[2], sqv.at[6], 14, sib_dev)

    def add_preact(j, fresh):
        @pl.loop(0, 2)
        def _(h):
            part = pl.ds(pl.multiple_of(h * half, half), half)
            value = contract_last(ag[j, part, :], bb[j])
            preact[part, :] = value if fresh else preact[part, :] + value

    add_preact(r, True)

    sq_s.wait_recv()
    sqv[3] = sqv[2] + sqv[6]
    sq_z = [send(sqv.at[3], sqv.at[6 + k], 14 + k, z_to[k]) for k in hops]

    remote(ag.at[rx, upper], ag.at[rx, upper], 8, x_dev).wait_recv()
    put(ag.at[rx], ag_out.at[rx], 3)
    add_preact(rx, False)
    remote(ag.at[ry, lower], ag.at[ry, lower], 9, y_dev).wait_recv()
    put(ag.at[ry], ag_out.at[ry], 4)
    add_preact(ry, False)

    whole = sqv[3]
    for k, copy in zip(hops, sq_z):
        copy.wait_recv()
        whole = whole + sqv[6 + k]
    factor = jnp.minimum(1.0, max_norm / jnp.sqrt(whole[0:1, 0:1] + 1e-06))

    @pl.loop(0, 2)
    def _(h):
        part = pl.ds(pl.multiple_of(h * half, half), half)
        clipped = factor * corr[part, :]
        new_mom = MOMENT_DECAY * mv[part, :] + clipped
        mv[part, :] = new_mom
        av[part, :] = av[part, :] - OUTER_RATE * (MOMENT_DECAY * new_mom + clipped)

    put(mv, new_mom_out, 0)
    put(av, new_anchor_out, 6)

    in_cot.wait()
    gram_high = gram[...].astype(jnp.bfloat16)
    gram_low = (gram[...] - gram_high.astype(jnp.float32)).astype(jnp.bfloat16)

    remote(ag.at[rd, lower], ag.at[rd, lower], 10, y_dev).wait_recv()
    remote(ag.at[rd, upper], ag.at[rd, upper], 11, x_dev).wait_recv()
    put(ag.at[rd], ag_out.at[rd], 5)
    add_preact(rd, False)

    @pl.loop(0, 2)
    def _(h):
        part = pl.ds(pl.multiple_of(h * half, half), half)
        first = preact[part, pl.ds(0, n_tok)] / root_width
        scaled = (cv[0, part, :].astype(jnp.float32) * silu_slope(first)).astype(jnp.bfloat16)
        moved = jnp.dot(scaled, gram_high, preferred_element_type=jnp.float32)
        moved = moved + jnp.dot(scaled, gram_low, preferred_element_type=jnp.float32)
        second = (1.0 - INNER_DECAY) * preact[part, pl.ds(n_tok, n_tok)]
        second = (second - INNER_RATE * (moved / root_width)) / root_width
        later = (cv[1, part, :].astype(jnp.float32) * silu_slope(second)).astype(jnp.bfloat16)
        coef = (1.0 - INNER_DECAY) * jnp.dot(
            scaled, selb[:, 0, :, :].reshape(n_tok, n_tok), preferred_element_type=jnp.float32
        )
        coef = coef + jnp.dot(
            later, selb[:, 1, :, :].reshape(n_tok, n_tok), preferred_element_type=jnp.float32
        )
        coef_out[part, :] = ((INNER_RATE / root_width) * coef).astype(jnp.bfloat16)

    for copy in started:
        copy.wait_send()
    for copy in pool_moves:
        copy.wait_send()
    for copy in outs:
        copy.wait()


def update_kernel(
    ag_ref, pool_ref, coef_ref, mom_ref, anchor_ref,
    delta_ref, new_anchor_ref, new_mom_ref,
):
    width = ag_ref.shape[2]
    keep = 1.0 - INNER_DECAY
    for b in range(2):
        rows = pool_ref[:, b, :, :].reshape(coef_ref.shape[1], width)
        moved = jnp.dot(coef_ref[...], rows, preferred_element_type=jnp.float32)
        value = (1.0 - keep * keep) * ag_ref[b].astype(jnp.float32) + moved
        delta_ref[0, :, width * b : width * (b + 1)] = value.astype(jnp.bfloat16)
    new_mom_ref[...] = mom_ref[...]
    new_anchor_ref[...] = anchor_ref[...]


def fast_body(anchor, prev_delta, momentum, pool, ids, cotangent):
    n_fsdp = lax.axis_size("fsdp")
    rows, width = anchor.shape
    full = prev_delta.shape[2]
    tok = pool.shape[1]
    n_tok = tok * n_fsdp
    half = rows // 2
    n_line = n_fsdp // 2
    bf16, f32 = jnp.bfloat16, jnp.float32
    hbm_spec = pl.BlockSpec(memory_space=pltpu.HBM)
    vmem_spec = pl.BlockSpec(memory_space=pltpu.VMEM)
    dma = pltpu.SemaphoreType.DMA
    ag, rows_all, moved_mom, moved_anchor, coef = pl.pallas_call(
        functools.partial(exchange_kernel, n_fsdp, CLIP_SHARE * math.sqrt(D * HW)),
        out_shape=(
            jax.ShapeDtypeStruct((4, rows, width), bf16),
            jax.ShapeDtypeStruct((n_fsdp, 4, tok, width), bf16),
            jax.ShapeDtypeStruct((rows, width), f32),
            jax.ShapeDtypeStruct((rows, width), f32),
            jax.ShapeDtypeStruct((rows, n_tok), bf16),
        ),
        in_specs=[vmem_spec] + [hbm_spec] * 5,
        out_specs=(hbm_spec, hbm_spec, hbm_spec, hbm_spec, vmem_spec),
        scratch_shapes=[
            pltpu.VMEM((rows, full), bf16),
            pltpu.VMEM((4, rows, width), bf16),
            pltpu.VMEM((rows, width), f32),
            pltpu.VMEM((rows, width), f32),
            pltpu.VMEM((tok, full), bf16),
            pltpu.VMEM((2, rows, n_tok), bf16),
            pltpu.VMEM((4, rows, width), bf16),
            pltpu.VMEM((n_fsdp, 4, tok, width), bf16),
            pltpu.VMEM((n_fsdp, 2, tok, n_tok), bf16),
            pltpu.VMEM((4, 2 * n_tok, width), bf16),
            pltpu.VMEM((2, half, width), bf16),
            pltpu.VMEM((2, half, width), bf16),
            pltpu.VMEM((2, half, width), bf16),
            pltpu.VMEM((2, half, width), bf16),
            pltpu.VMEM((rows, width), f32),
            pltpu.VMEM((rows, 2 * n_tok), f32),
            pltpu.VMEM((n_tok, n_tok), f32),
            pltpu.VMEM((6 + n_line, 8, 128), f32),
            dma((6,)),
            dma((7,)),
            dma((14 + n_line,)),
            dma((14 + n_line,)),
            dma((2 * n_line,)),
            dma((2 * n_line,)),
            dma((2 * n_line,)),
            dma((2 * n_line,)),
        ],
        compiler_params=pltpu.CompilerParams(
            collective_id=0, has_side_effects=True, vmem_limit_bytes=63 * 1024 * 1024
        ),
        name="exchange",
    )(ids, prev_delta, anchor, momentum, pool, cotangent)
    quarter = rows // 4
    by_rows = pl.BlockSpec((quarter, width), lambda c, i: (2 * c + i, 0))
    delta, new_anchor, new_momentum = pl.pallas_call(
        update_kernel,
        grid=(2, 2),
        out_shape=(
            jax.ShapeDtypeStruct(prev_delta.shape, bf16),
            jax.ShapeDtypeStruct(anchor.shape, f32),
            jax.ShapeDtypeStruct(anchor.shape, f32),
        ),
        in_specs=[
            pl.BlockSpec((2, half, width), lambda c, i: (c, i, 0)),
            pl.BlockSpec((n_fsdp, 2, tok, width), lambda c, i: (0, c, 0, 0)),
            pl.BlockSpec((half, n_tok), lambda c, i: (i, 0)),
            by_rows,
            by_rows,
        ],
        out_specs=(
            pl.BlockSpec((1, half, 2 * width), lambda c, i: (0, i, c)),
            by_rows,
            by_rows,
        ),
        compiler_params=pltpu.CompilerParams(vmem_limit_bytes=63 * 1024 * 1024),
        name="update",
    )(ag, rows_all, coef, moved_mom, moved_anchor)
    return (delta, new_anchor, new_momentum)


def body(anchor, prev_delta, momentum, pool, ids, cotangent):
    rows, width = anchor.shape
    fits = (
        lax.axis_size("replica") == 4
        and lax.axis_size("fsdp") % 2 == 0
        and rows % 32 == 0
        and width % 64 == 0
        and pool.shape[1] % 16 == 0
        and ids.shape[1] == 2
        and ids.shape[2] == pool.shape[1]
        and (ids.shape[2] * lax.axis_size("fsdp")) % 128 == 0
    )
    chosen = fast_body if fits else plain_body
    return chosen(anchor, prev_delta, momentum, pool, ids, cotangent)


def solution(mesh):
    return jax.shard_map(
        body,
        mesh=mesh,
        in_specs=(
            P("fsdp", "replica"),
            P("replica", "fsdp", None),
            P("fsdp", "replica"),
            P("replica", "fsdp", None),
            P("replica", None, "fsdp"),
            P("replica", None, "fsdp", None),
        ),
        out_specs=(P("replica", "fsdp", None), P("fsdp", "replica"), P("fsdp", "replica")),
        check_vma=False,
    )
```
